32 devices in a mesh: groups: 2 (over x), dp: 8 (over z, y), tensor: 2 (over core).
Axes of the slice: x: 2, y: 2, z: 4, core: 2. Of those that a mesh axis runs over, the one named last changes fastest.
Arguments:
- hidden: bfloat16 [2048, 8192], P(('groups', 'dp'), 'tensor'), parts along dimension 0, may hold values from -6 to 6
- row_adapter_index: int32 [2048, 1], P(('groups', 'dp')), parts along dimension 0, may hold values from 0 to 15; in each aligned block of 128 rows (0 to 127, 128 to 255, ...) at most 16 rows name the same one
- key_value_weight: bfloat16 [8192, 2048], P('tensor'), may hold values from -0.0625 to 0.0625
- adapter_down_weight: bfloat16 [32, 8192, 128], P(('groups', 'dp'), 'tensor'), parts along dimension 0, may hold values from -0.0625 to 0.0625
- adapter_up_weight: bfloat16 [32, 2, 64, 1024], P(('groups', 'dp')), parts along dimension 0, may hold values from -0.75 to 0.75
Outputs:
- new_kv: bfloat16 [2048, 2048], P(('groups', 'dp'), 'tensor'), parts along dimension 0
The draws below stay inside these ranges and needn't reach their ends.
There are 2 independent parts, one for each index of `groups`. The reference program is written for one: setup_inputs(seed, part) draws one part's arguments, and reference() takes and returns one part's arrays. A program takes and returns all parts, laid end to end along the dimension named above; an argument that names none is the same for every part. Nothing has to cross between parts.
Inputs may be any that keep to these rules, and one draw needn't show every extreme that they name: `row_adapter_index`: within the 128 rows of one dp index (aligned blocks of rows), no adapter is named by more than 16 rows, a bound that some block reaches.
All inputs are finite; a program needn't handle non-finite values.
Results may differ from the reference program's by a relative error of at most 0.001.
Values may be sent and summed in bfloat16 or wider, within the bound.
A program may use at most 64 MiB of HBM per device.

```python
import math
import jax
import jax.numpy as jnp
import numpy as np
from jax import lax

MODEL_WIDTH = 8192
ADAPTER_RANK = 64
R_DEV = 128
KEY_VALUE_WIDTH = 1024
CAP = 16
ADAPTER_COUNT = 16
ROWS = 1024


def block_levels(own_key, dims, shards, low, largest):
    def one(axis_at, blocks):
        heights = jax.random.uniform(jax.random.fold_in(jax.random.fold_in(own_key, 6), axis_at), (blocks,), jnp.float32, low / len(shards), largest / len(shards))
        return jnp.repeat(jnp.exp(heights), dims[axis_at] // blocks).reshape((-1,) + (1,) * (len(dims) - axis_at - 1))

    gain = one(*shards[0])
    for cut in shards[1:]:
        gain = gain * one(*cut)
    return gain


def shared_out(stream_key, own, number, rows, count, top, limit, skew):
    ranking = jax.random.permutation(stream_key, count)
    heavy_load, common = load_shares(count, rows * top, limit, skew, True), load_shares(count, rows * top, limit, skew, False)
    places = jnp.arange(count)

    def named(tallies, rotation):
        used = int((tallies > 0).sum())
        fixed = max(1, used // 4)
        shifted = fixed + (places - fixed + rotation * (used - fixed)) % max(1, count - fixed)
        return jnp.zeros((count,), jnp.int32).at[ranking[jnp.where(places < fixed, places, shifted)]].set(jnp.asarray(tallies, jnp.int32))

    tallies = jnp.where(number % 4 == 0, named(heavy_load, number // 4), named(common, number - number // 4 - 1))
    mixed = jax.random.permutation(jax.random.fold_in(own, 3), count)
    giver, receiver = mixed[0:count // 2 * 2:2], mixed[1:count // 2 * 2:2]
    room = jnp.minimum(tallies[giver] - 1, limit - tallies[receiver]) // 2
    room = jnp.where((giver == ranking[0]) | (receiver == ranking[0]) | (tallies[receiver] == 0), 0, jnp.maximum(room, 0))
    shifted = jax.random.randint(jax.random.fold_in(own, 4), (count // 2,), 0, 1 << 20) % (room + 1)
    tallies = tallies.at[giver].add(-shifted).at[receiver].add(shifted)
    members = jnp.searchsorted(jnp.cumsum(tallies), jnp.arange(rows * top), side="right").astype(jnp.int32)
    listing = members.reshape(top, rows).T
    listing = listing[jax.random.permutation(jax.random.fold_in(own, 1), rows)]
    rotation = jax.random.randint(jax.random.fold_in(own, 2), (rows, 1), 0, top)
    return jnp.take_along_axis(listing, (jnp.arange(top)[None, :] + rotation) % top, axis=1)


def load_shares(count, total, limit, skew, full):
    portions = [(1 << 20) // math.isqrt(standing ** skew) + 1 for standing in range(1, count + 1)]
    largest = limit if full else min(limit, max(-(-total // count), total * portions[0] // sum(portions)))
    least = 1 if total - largest >= count - 1 else 0
    holding, surplus = [largest] + [least] * (count - 1), total - largest - least * (count - 1)
    while surplus > 0:
        free = [i for i in range(1, count) if holding[i] < largest] or [i for i in range(1, count) if holding[i] < limit]
        pool, budget = sum([portions[i] for i in free]), surplus
        for i in free:
            extra = min(limit - holding[i], max(1, budget * portions[i] // pool), surplus)
            holding[i] = holding[i] + extra
            surplus = surplus - extra
    return np.array(holding)


def normal_values(key, shape, scale, bound, split=(), held_as=jnp.bfloat16):
    gain = block_levels(key, shape, split, -0.22, 0.18) if split else 1.0
    entries = jax.random.normal(key, shape, jnp.float32) * scale * gain
    return jnp.minimum(jnp.maximum(entries, -bound), bound).astype(held_as)


def setup_inputs(seed: int = 0, part: int = 0) -> dict:
    splits = jax.random.split(jax.random.key(seed), 6)
    part_splits = jax.random.split(jax.random.fold_in(splits[5], part), 6)
    hidden = normal_values(part_splits[0], (ROWS, MODEL_WIDTH), 1.0, 6.0, ((0, 8), (1, 2)))
    row_adapter_index_keys = jax.random.split(jax.random.fold_in(part_splits[1], 1), ROWS // R_DEV)
    row_adapter_index_turns = jax.random.permutation(jax.random.fold_in(part_splits[1], 3), ROWS // R_DEV)
    row_adapter_index = jax.vmap(lambda own, number: shared_out(jax.random.fold_in(part_splits[1], 2), own, number, R_DEV, ADAPTER_COUNT, 1, CAP, 2))(row_adapter_index_keys, row_adapter_index_turns).reshape((ROWS, 1))
    key_value_weight = normal_values(splits[2], (MODEL_WIDTH, 2 * KEY_VALUE_WIDTH), MODEL_WIDTH ** -0.5, 0.0625, ((0, 2),))
    adapter_down_weight = normal_values(part_splits[3], (ADAPTER_COUNT, MODEL_WIDTH, 2 * ADAPTER_RANK), MODEL_WIDTH ** -0.5, 0.0625, ((0, 8), (1, 2)))
    adapter_up_weight = normal_values(part_splits[4], (ADAPTER_COUNT, 2, ADAPTER_RANK, KEY_VALUE_WIDTH), ADAPTER_RANK ** -0.5, 0.75, ((0, 8),))
    return {"hidden": hidden, "row_adapter_index": row_adapter_index, "key_value_weight": key_value_weight, "adapter_down_weight": adapter_down_weight, "adapter_up_weight": adapter_up_weight}


def reference(hidden, row_adapter_index, key_value_weight, adapter_down_weight, adapter_up_weight):
    base_output = jnp.dot(hidden, key_value_weight, preferred_element_type=jnp.float32)

    def single_row_input(row_item):
        row_vector, chosen_adapter = row_item
        down_weight = lax.dynamic_index_in_dim(adapter_down_weight, chosen_adapter, 0, keepdims=False)
        shrink = jnp.dot(row_vector[None, :], down_weight, preferred_element_type=jnp.float32)[0]
        up_weight = lax.dynamic_index_in_dim(adapter_up_weight, chosen_adapter, 0, keepdims=False).astype(jnp.float32)
        key_part = jnp.dot(shrink[:ADAPTER_RANK], up_weight[0], precision=lax.Precision.HIGHEST)
        value_part = jnp.dot(shrink[ADAPTER_RANK:], up_weight[1], precision=lax.Precision.HIGHEST)
        return jnp.concatenate([key_part, value_part])

    adapter_delta = lax.map(single_row_input, (hidden, row_adapter_index[:, 0].astype(jnp.int32)))
    return (base_output + adapter_delta).astype(jnp.bfloat16)
```

```python
import functools

import jax
import jax.numpy as jnp
from jax import lax
from jax.experimental import pallas as pl
from jax.experimental.pallas import tpu as pltpu
from jax.sharding import PartitionSpec as P

CAP = 16
MESH = pl.DeviceIdType.MESH
FEATURE_CHUNKS = 4
WEIGHT_CHUNKS = 8


def partner(me, offset):
    other, bit = me, 1
    while bit <= offset:
        if offset & bit:
            other = other + bit - 2 * bit * ((me // bit) % 2)
        bit *= 2
    return other


def kernel(
    n, index_ref, hidden_hbm, weight_hbm, down_hbm, up_hbm, out_ref,
    hidden, weight, down, up, packed, arrived, total, base_arrived, shrink, shrink_out, shrink_in,
    load_hidden, load_weight, load_down, load_up,
    row_send, row_recv, up_send, up_recv, back_send, back_recv, base_send, base_recv,
):
    me = lax.axis_index("dp")
    core = lax.axis_index("tensor")
    sibling = 1 - core
    rows, width = hidden.shape
    adapters = down.shape[0]
    rank = up_hbm.shape[2]
    lanes = up.shape[2]
    chunk = width // FEATURE_CHUNKS
    depth = width // WEIGHT_CHUNKS
    slots = adapters * CAP

    def hidden_load(c):
        part = pl.ds(c * chunk, chunk)
        return pltpu.make_async_copy(hidden_hbm.at[:, part], hidden.at[:, part], load_hidden.at[c])

    def weight_load(k):
        part = pl.ds(k * depth, depth)
        return pltpu.make_async_copy(weight_hbm.at[part], weight.at[part], load_weight.at[k])

    def up_load(j):
        return pltpu.make_async_copy(
            up_hbm.at[j, core], up.at[me, pl.ds(j * rank, rank)], load_up.at[j]
        )

    down_load = pltpu.make_async_copy(down_hbm, down, load_down)
    for c in range(FEATURE_CHUNKS):
        hidden_load(c).start()
    for j in range(adapters):
        up_load(j).start()
    for k in range(WEIGHT_CHUNKS):
        weight_load(k).start()
    down_load.start()

    barrier = pltpu.get_barrier_semaphore()
    for offset in range(n):
        for other in range(2):
            if offset or other:
                pl.semaphore_signal(
                    barrier, inc=1, device_id_type=MESH,
                    device_id={"dp": partner(me, offset), "tensor": sibling if other else core},
                )

    chosen = index_ref[...]
    one_hot = chosen == lax.broadcasted_iota(jnp.int32, (rows, adapters * n), 1)
    one_hot = jnp.where(one_hot, 1.0, 0.0)
    below = lax.broadcasted_iota(jnp.int32, (rows, rows), 0) > lax.broadcasted_iota(
        jnp.int32, (rows, rows), 1
    )
    earlier = jnp.dot(
        jnp.where(below, 1.0, 0.0).astype(jnp.bfloat16), one_hot.astype(jnp.bfloat16),
        preferred_element_type=jnp.float32,
    )
    position = jnp.sum(earlier * one_hot, axis=1, keepdims=True).astype(jnp.int32)
    slot = chosen * CAP + position
    placement = jnp.where(
        slot == lax.broadcasted_iota(jnp.int32, (rows, n * slots), 1), 1.0, 0.0
    ).T.astype(jnp.bfloat16)

    for j in range(adapters):
        up_load(j).wait()
    pl.semaphore_wait(barrier, 2 * n - 1)

    def up_copy(offset, step):
        block = partner(me, offset ^ step)
        return pltpu.make_async_remote_copy(
            src_ref=up.at[block], dst_ref=up.at[block],
            send_sem=up_send.at[offset], recv_sem=up_recv.at[offset],
            device_id={"dp": partner(me, step)}, device_id_type=MESH,
        )

    def up_arrival(offset):
        block = up.at[partner(me, offset)]
        return pltpu.make_async_remote_copy(
            src_ref=block, dst_ref=block,
            send_sem=up_send.at[offset], recv_sem=up_recv.at[offset],
            device_id={"dp": partner(me, 1)}, device_id_type=MESH,
        )

    steps = []
    step = n // 2
    while step:
        steps.append((step, [step + held for held in range(0, n, 2 * step)]))
        step //= 2

    def up_start(number):
        step, offsets = steps[number]
        for offset in offsets:
            up_copy(offset, step).start()

    def up_wait(number):
        for offset in steps[number][1]:
            up_arrival(offset).wait_recv()

    order = sorted(range(1, n), reverse=True)

    def row_copy(c, offset):
        target = partner(me, offset)
        return pltpu.make_async_remote_copy(
            src_ref=packed.at[c, target], dst_ref=arrived.at[c, me],
            send_sem=row_send.at[c, offset], recv_sem=row_recv.at[c, offset],
            device_id={"dp": target}, device_id_type=MESH,
        )

    def row_arrival(c, offset):
        return pltpu.make_async_remote_copy(
            src_ref=packed.at[c, 0], dst_ref=arrived.at[c, partner(me, offset)],
            send_sem=row_send.at[c, offset], recv_sem=row_recv.at[c, offset],
            device_id={"dp": partner(me, offset)}, device_id_type=MESH,
        )

    def rows_start(c):
        hidden_load(c).wait()
        block = jnp.dot(
            placement, hidden[:, c * chunk:(c + 1) * chunk], preferred_element_type=jnp.float32
        ).astype(jnp.bfloat16)
        packed[c] = block.reshape(n, slots, chunk)
        for offset in order:
            row_copy(c, offset).start()
        arrived[c, me] = packed[c, me]

    def rows_use(c):
        for offset in order:
            row_arrival(c, offset).wait_recv()
        for j in range(adapters):
            taken = arrived[c, :, j * CAP:(j + 1) * CAP, :].reshape(n * CAP, chunk)
            part = jnp.dot(
                taken, down[j, c * chunk:(c + 1) * chunk, :], preferred_element_type=jnp.float32
            )
            if c == 0:
                shrink[j] = part
            else:
                shrink[j] += part

    up_start(0)
    for c in range(FEATURE_CHUNKS):
        rows_start(c)

    for k in range(WEIGHT_CHUNKS):
        weight_load(k).wait()
        for half in range(2):
            part = jnp.dot(
                hidden[:, k * depth:(k + 1) * depth],
                weight[k * depth:(k + 1) * depth, half * lanes:(half + 1) * lanes],
                preferred_element_type=jnp.float32,
            )
            if k == 0:
                total[half] = part
            else:
                total[half] += part
    base_copy = pltpu.make_async_remote_copy(
        src_ref=total.at[sibling], dst_ref=base_arrived, send_sem=base_send, recv_sem=base_recv,
        device_id={"tensor": sibling}, device_id_type=MESH,
    )
    base_copy.start()

    down_load.wait()
    for number in range(len(steps) - 1):
        up_wait(number)
        up_start(number + 1)
    for c in range(FEATURE_CHUNKS):
        rows_use(c)

    for half in range(2):
        shrink_out[half] = jnp.concatenate(
            [shrink[j][:, half * rank:(half + 1) * rank] for j in range(adapters)], axis=1
        ).reshape(n, CAP, adapters * rank)

    def back_copy(offset, other):
        to_core = sibling if other else core
        target = partner(me, offset)
        return pltpu.make_async_remote_copy(
            src_ref=shrink_out.at[to_core, target], dst_ref=shrink_in.at[core, me],
            send_sem=back_send.at[other, offset], recv_sem=back_recv.at[other, offset],
            device_id={"dp": target, "tensor": to_core}, device_id_type=MESH,
        )

    def back_arrival(offset, other):
        from_core = sibling if other else core
        source = partner(me, offset)
        return pltpu.make_async_remote_copy(
            src_ref=shrink_out.at[0, 0], dst_ref=shrink_in.at[from_core, source],
            send_sem=back_send.at[other, offset], recv_sem=back_recv.at[other, offset],
            device_id={"dp": source, "tensor": from_core}, device_id_type=MESH,
        )

    back = [(offset, other) for offset in order + [0] for other in range(2) if offset or other]
    for offset, other in back:
        back_copy(offset, other).start()
    shrink_in[core, me] = shrink_out[core, me]

    base_copy.wait()
    summed = total[core] + base_arrived[...]
    up_wait(len(steps) - 1)
    for offset, other in back:
        back_arrival(offset, other).wait_recv()

    got = jnp.concatenate([shrink_in[0, d] + shrink_in[1, d] for d in range(n)], axis=1)
    high = got.astype(jnp.bfloat16)
    low = (got - high.astype(jnp.float32)).astype(jnp.bfloat16)
    pick = jnp.where(
        position == lax.broadcasted_iota(jnp.int32, (rows, CAP), 1), 1.0, 0.0
    ).astype(jnp.bfloat16)
    mine = lax.broadcasted_iota(jnp.int32, (rows, n * adapters * rank), 1) // rank == chosen

    def spread(values):
        taken = jnp.dot(pick, values, preferred_element_type=jnp.float32)
        return jnp.where(mine, taken, 0.0).astype(jnp.bfloat16)

    spread_rows = jnp.concatenate([spread(high), spread(low)], axis=0)
    delta = jnp.dot(
        spread_rows, up[...].reshape(n * adapters * rank, lanes), preferred_element_type=jnp.float32
    )
    out_ref[...] = (summed + (delta[:rows] + delta[rows:])).astype(out_ref.dtype)

    for number in range(len(steps)):
        step, offsets = steps[number]
        for offset in offsets:
            up_copy(offset, step).wait_send()
    for c in range(FEATURE_CHUNKS):
        for offset in order:
            row_copy(c, offset).wait_send()
    for offset, other in back:
        back_copy(offset, other).wait_send()


def per_device(hidden, row_adapter_index, key_value_weight, adapter_down_weight, adapter_up_weight):
    n = lax.axis_size("dp")
    rows, width = hidden.shape
    adapters, _, ranks = adapter_down_weight.shape
    _, _, rank, lanes = adapter_up_weight.shape
    slots = adapters * CAP
    chunk = width // FEATURE_CHUNKS
    hbm = pl.BlockSpec(memory_space=pl.ANY)
    vmem = pl.BlockSpec(memory_space=pltpu.VMEM)
    dma = pltpu.SemaphoreType.DMA
    return pl.pallas_call(
        functools.partial(kernel, n),
        out_shape=jax.ShapeDtypeStruct((rows, lanes), jnp.bfloat16),
        in_specs=[vmem, hbm, hbm, hbm, hbm],
        out_specs=vmem,
        scratch_shapes=[
            pltpu.VMEM((rows, width), jnp.bfloat16),
            pltpu.VMEM(key_value_weight.shape, jnp.bfloat16),
            pltpu.VMEM(adapter_down_weight.shape, jnp.bfloat16),
            pltpu.VMEM((n, adapters * rank, lanes), jnp.bfloat16),
            pltpu.VMEM((FEATURE_CHUNKS, n, slots, chunk), jnp.bfloat16),
            pltpu.VMEM((FEATURE_CHUNKS, n, slots, chunk), jnp.bfloat16),
            pltpu.VMEM((2, rows, lanes), jnp.float32),
            pltpu.VMEM((rows, lanes), jnp.float32),
            pltpu.VMEM((adapters, n * CAP, ranks), jnp.float32),
            pltpu.VMEM((2, n, CAP, adapters * rank), jnp.float32),
            pltpu.VMEM((2, n, CAP, adapters * rank), jnp.float32),
            dma((FEATURE_CHUNKS,)),
            dma((WEIGHT_CHUNKS,)),
            dma,
            dma((adapters,)),
            dma((FEATURE_CHUNKS, n)),
            dma((FEATURE_CHUNKS, n)),
            dma((n,)),
            dma((n,)),
            dma((2, n)),
            dma((2, n)),
            dma,
            dma,
        ],
        compiler_params=pltpu.CompilerParams(
            collective_id=0, has_side_effects=True, vmem_limit_bytes=56 * 1024 * 1024
        ),
        cost_estimate=pl.CostEstimate(
            flops=2 * rows * width * 2 * lanes, bytes_accessed=20 * 1024 * 1024, transcendentals=0
        ),
    )(row_adapter_index, hidden, key_value_weight, adapter_down_weight, adapter_up_weight)


def solution(mesh):
    in_specs = (
        P(("groups", "dp"), "tensor"),
        P(("groups", "dp"), None),
        P("tensor", None),
        P(("groups", "dp"), "tensor", None),
        P(("groups", "dp"), None, None, None),
    )
    out_specs = P(("groups", "dp"), "tensor")
    return jax.shard_map(
        per_device, mesh=mesh, in_specs=in_specs, out_specs=out_specs, check_vma=False
    )
```

```python
import functools

import jax
import jax.numpy as jnp
from jax import lax
from jax.experimental import pallas as pl
from jax.experimental.pallas import tpu as pltpu
from jax.sharding import PartitionSpec as P

CAP = 16
MESH = pl.DeviceIdType.MESH
FEATURE_CHUNKS = 4
WEIGHT_CHUNKS = 8


def partner(me, offset):
    other, bit = me, 1
    while bit <= offset:
        if offset & bit:
            other = other + bit - 2 * bit * ((me // bit) % 2)
        bit *= 2
    return other


def kernel(
    n, index_ref, hidden_hbm, weight_hbm, down_hbm, up_hbm, out_ref,
    hidden, weight, down, up, packed, arrived, total, base_arrived, shrink, shrink_out, shrink_in,
    load_hidden, load_weight, load_down, load_up,
    row_send, row_recv, up_send, up_recv, back_send, back_recv, base_send, base_recv,
):
    me = lax.axis_index("dp")
    core = lax.axis_index("tensor")
    sibling = 1 - core
    rows, width = hidden.shape
    adapters = down.shape[0]
    rank = up_hbm.shape[2]
    lanes = up.shape[2]
    chunk = width // FEATURE_CHUNKS
    depth = width // WEIGHT_CHUNKS
    slots = adapters * CAP

    def hidden_load(c):
        part = pl.ds(c * chunk, chunk)
        return pltpu.make_async_copy(hidden_hbm.at[:, part], hidden.at[:, part], load_hidden.at[c])

    def weight_load(k):
        part = pl.ds(k * depth, depth)
        return pltpu.make_async_copy(weight_hbm.at[part], weight.at[part], load_weight.at[k])

    def up_load(j):
        return pltpu.make_async_copy(
            up_hbm.at[j, core], up.at[me, pl.ds(j * rank, rank)], load_up.at[j]
        )

    down_load = pltpu.make_async_copy(down_hbm, down, load_down)
    for c in range(FEATURE_CHUNKS):
        hidden_load(c).start()
    for j in range(adapters):
        up_load(j).start()
    for k in range(WEIGHT_CHUNKS):
        weight_load(k).start()
    down_load.start()

    barrier = pltpu.get_barrier_semaphore()
    for offset in range(n):
        for other in range(2):
            if offset or other:
                pl.semaphore_signal(
                    barrier, inc=1, device_id_type=MESH,
                    device_id={"dp": partner(me, offset), "tensor": sibling if other else core},
                )

    row_at = lax.broadcasted_iota(jnp.int32, (rows, rows), 0)
    column_at = lax.broadcasted_iota(jnp.int32, (rows, rows), 1)
    chosen = jnp.sum(
        jnp.where(row_at == column_at, index_ref[...], 0), axis=1, keepdims=True
    )
    one_hot = chosen == lax.broadcasted_iota(jnp.int32, (rows, adapters * n), 1)
    one_hot = jnp.where(one_hot, 1.0, 0.0)
    earlier = jnp.dot(
        jnp.where(row_at > column_at, 1.0, 0.0).astype(jnp.bfloat16), one_hot.astype(jnp.bfloat16),
        preferred_element_type=jnp.float32,
    )
    position = jnp.sum(earlier * one_hot, axis=1, keepdims=True).astype(jnp.int32)
    slot = chosen * CAP + position
    placement = jnp.where(
        slot == lax.broadcasted_iota(jnp.int32, (rows, n * slots), 1), 1.0, 0.0
    ).T.astype(jnp.bfloat16)

    for j in range(adapters):
        up_load(j).wait()
    pl.semaphore_wait(barrier, 2 * n - 1)

    def up_copy(offset, step):
        block = partner(me, offset ^ step)
        return pltpu.make_async_remote_copy(
            src_ref=up.at[block], dst_ref=up.at[block],
            send_sem=up_send.at[offset], recv_sem=up_recv.at[offset],
            device_id={"dp": partner(me, step)}, device_id_type=MESH,
        )

    def up_arrival(offset):
        block = up.at[partner(me, offset)]
        return pltpu.make_async_remote_copy(
            src_ref=block, dst_ref=block,
            send_sem=up_send.at[offset], recv_sem=up_recv.at[offset],
            device_id={"dp": partner(me, 1)}, device_id_type=MESH,
        )

    levels = [[] for _ in range(n.bit_length() - 1)]
    for offset in reversed(range(0, n, 2)):
        levels[offset.bit_count()].append(offset)

    def up_forward(held):
        last = held & -held if held else n
        return [(held + step, step) for step in (2 ** e for e in reversed(range(n))) if step < last]

    def up_level(number):
        for held in levels[number]:
            if held:
                up_arrival(held).wait_recv()
            for offset, step in up_forward(held):
                up_copy(offset, step).start()

    order = sorted(range(1, n), reverse=True)

    def row_copy(c, offset):
        target = partner(me, offset)
        return pltpu.make_async_remote_copy(
            src_ref=packed.at[c, target], dst_ref=arrived.at[c, me],
            send_sem=row_send.at[c, offset], recv_sem=row_recv.at[c, offset],
            device_id={"dp": target}, device_id_type=MESH,
        )

    def row_arrival(c, offset):
        return pltpu.make_async_remote_copy(
            src_ref=packed.at[c, 0], dst_ref=arrived.at[c, partner(me, offset)],
            send_sem=row_send.at[c, offset], recv_sem=row_recv.at[c, offset],
            device_id={"dp": partner(me, offset)}, device_id_type=MESH,
        )

    def rows_start(c):
        hidden_load(c).wait()
        block = jnp.dot(
            placement, hidden[:, c * chunk:(c + 1) * chunk], preferred_element_type=jnp.float32
        ).astype(jnp.bfloat16)
        packed[c] = block.reshape(n, slots, chunk)
        for offset in order:
            row_copy(c, offset).start()
        arrived[c, me] = packed[c, me]

    def rows_use(c):
        for offset in order:
            row_arrival(c, offset).wait_recv()
        for j in range(adapters):
            taken = arrived[c, :, j * CAP:(j + 1) * CAP, :].reshape(n * CAP, chunk)
            part = jnp.dot(
                taken, down[j, c * chunk:(c + 1) * chunk, :], preferred_element_type=jnp.float32
            )
            if c == 0:
                shrink[j] = part
            else:
                shrink[j] += part

    def base():
        for k in range(WEIGHT_CHUNKS):
            weight_load(k).wait()
            for half in range(2):
                part = jnp.dot(
                    hidden[:, k * depth:(k + 1) * depth],
                    weight[k * depth:(k + 1) * depth, half * lanes:(half + 1) * lanes],
                    preferred_element_type=jnp.float32,
                )
                if k == 0:
                    total[half] = part
                else:
                    total[half] += part
        base_copy.start()

    base_copy = pltpu.make_async_remote_copy(
        src_ref=total.at[sibling], dst_ref=base_arrived, send_sem=base_send, recv_sem=base_recv,
        device_id={"tensor": sibling}, device_id_type=MESH,
    )
    up_level(0)
    for c in range(FEATURE_CHUNKS):
        rows_start(c)
    base()
    down_load.wait()
    for number in range(1, len(levels)):
        up_level(number)
    for c in range(FEATURE_CHUNKS):
        rows_use(c)

    for half in range(2):
        shrink_out[half] = jnp.concatenate(
            [shrink[j][:, half * rank:(half + 1) * rank] for j in range(adapters)], axis=1
        ).reshape(n, CAP, adapters * rank)

    def back_copy(offset, other):
        to_core = sibling if other else core
        target = partner(me, offset)
        return pltpu.make_async_remote_copy(
            src_ref=shrink_out.at[to_core, target], dst_ref=shrink_in.at[core, me],
            send_sem=back_send.at[other, offset], recv_sem=back_recv.at[other, offset],
            device_id={"dp": target, "tensor": to_core}, device_id_type=MESH,
        )

    def back_arrival(offset, other):
        from_core = sibling if other else core
        source = partner(me, offset)
        return pltpu.make_async_remote_copy(
            src_ref=shrink_out.at[0, 0], dst_ref=shrink_in.at[from_core, source],
            send_sem=back_send.at[other, offset], recv_sem=back_recv.at[other, offset],
            device_id={"dp": source, "tensor": from_core}, device_id_type=MESH,
        )

    back = [(offset, other) for offset in order + [0] for other in range(2) if offset or other]
    for offset, other in back:
        back_copy(offset, other).start()
    shrink_in[core, me] = shrink_out[core, me]

    base_copy.wait()
    summed = total[core] + base_arrived[...]
    for offset in range(1, n, 2):
        up_arrival(offset).wait_recv()
    for offset, other in back:
        back_arrival(offset, other).wait_recv()

    got = jnp.concatenate([shrink_in[0, d] + shrink_in[1, d] for d in range(n)], axis=1)
    high = got.astype(jnp.bfloat16)
    low = (got - high.astype(jnp.float32)).astype(jnp.bfloat16)
    pick = jnp.where(
        position == lax.broadcasted_iota(jnp.int32, (rows, CAP), 1), 1.0, 0.0
    ).astype(jnp.bfloat16)
    mine = lax.broadcasted_iota(jnp.int32, (rows, n * adapters * rank), 1) // rank == chosen

    def spread(values):
        taken = jnp.dot(pick, values, preferred_element_type=jnp.float32)
        return jnp.where(mine, taken, 0.0).astype(jnp.bfloat16)

    spread_rows = jnp.concatenate([spread(high), spread(low)], axis=0)
    delta = jnp.dot(
        spread_rows, up[...].reshape(n * adapters * rank, lanes), preferred_element_type=jnp.float32
    )
    out_ref[...] = (summed + (delta[:rows] + delta[rows:])).astype(out_ref.dtype)

    for held in range(n):
        for offset, step in up_forward(held):
            up_copy(offset, step).wait_send()
    for c in range(FEATURE_CHUNKS):
        for offset in order:
            row_copy(c, offset).wait_send()
    for offset, other in back:
        back_copy(offset, other).wait_send()


def per_device(hidden, row_adapter_index, key_value_weight, adapter_down_weight, adapter_up_weight):
    n = lax.axis_size("dp")
    rows, width = hidden.shape
    adapters, _, ranks = adapter_down_weight.shape
    _, _, rank, lanes = adapter_up_weight.shape
    slots = adapters * CAP
    chunk = width // FEATURE_CHUNKS
    hbm = pl.BlockSpec(memory_space=pl.ANY)
    vmem = pl.BlockSpec(memory_space=pltpu.VMEM)
    dma = pltpu.SemaphoreType.DMA
    return pl.pallas_call(
        functools.partial(kernel, n),
        out_shape=jax.ShapeDtypeStruct((rows, lanes), jnp.bfloat16),
        in_specs=[vmem, hbm, hbm, hbm, hbm],
        out_specs=vmem,
        scratch_shapes=[
            pltpu.VMEM((rows, width), jnp.bfloat16),
            pltpu.VMEM(key_value_weight.shape, jnp.bfloat16),
            pltpu.VMEM(adapter_down_weight.shape, jnp.bfloat16),
            pltpu.VMEM((n, adapters * rank, lanes), jnp.bfloat16),
            pltpu.VMEM((FEATURE_CHUNKS, n, slots, chunk), jnp.bfloat16),
            pltpu.VMEM((FEATURE_CHUNKS, n, slots, chunk), jnp.bfloat16),
            pltpu.VMEM((2, rows, lanes), jnp.float32),
            pltpu.VMEM((rows, lanes), jnp.float32),
            pltpu.VMEM((adapters, n * CAP, ranks), jnp.float32),
            pltpu.VMEM((2, n, CAP, adapters * rank), jnp.float32),
            pltpu.VMEM((2, n, CAP, adapters * rank), jnp.float32),
            dma((FEATURE_CHUNKS,)),
            dma((WEIGHT_CHUNKS,)),
            dma,
            dma((adapters,)),
            dma((FEATURE_CHUNKS, n)),
            dma((FEATURE_CHUNKS, n)),
            dma((n,)),
            dma((n,)),
            dma((2, n)),
            dma((2, n)),
            dma,
            dma,
        ],
        compiler_params=pltpu.CompilerParams(
            collective_id=0, has_side_effects=True, vmem_limit_bytes=56 * 1024 * 1024
        ),
        cost_estimate=pl.CostEstimate(
            flops=2 * rows * width * 2 * lanes, bytes_accessed=20 * 1024 * 1024, transcendentals=0
        ),
    )(row_adapter_index.reshape(1, rows), hidden, key_value_weight, adapter_down_weight, adapter_up_weight)


def solution(mesh):
    in_specs = (
        P(("groups", "dp"), "tensor"),
        P(("groups", "dp"), None),
        P("tensor", None),
        P(("groups", "dp"), "tensor", None),
        P(("groups", "dp"), None, None, None),
    )
    out_specs = P(("groups", "dp"), "tensor")
    return jax.shard_map(
        per_device, mesh=mesh, in_specs=in_specs, out_specs=out_specs, check_vma=False
    )
```
